512 devices in a mesh: dp: 4 (over x), expert: 128 (over y, z, core).
Axes of the slice: x: 4, y: 8, z: 8, core: 2. Of those that a mesh axis runs over, the one named last changes fastest.
Arguments:
- out_grad: bfloat16 [8192, 1536], P(('dp', 'expert')), may hold values from -1.5 to 1.5
- routes: int32 [8192, 8], P(('dp', 'expert')), may hold values from 0 to 127, all different within a row; in each aligned block of 16 rows (0 to 15, 16 to 31, ...) at most 2 rows name the same one
- gate_probs: float32 [8192, 8], P(('dp', 'expert')), may hold values from 0.05 to 1
- saved_inputs: bfloat16 [4, 128, 256, 1536], P('dp', 'expert'), may hold values from -6 to 6
- w_gate: bfloat16 [128, 1536, 384], P('expert', 'dp'), may hold values from -0.15625 to 0.15625
- w_up: bfloat16 [128, 1536, 384], P('expert', 'dp'), may hold values from -0.15625 to 0.15625
- w_down: bfloat16 [128, 1536, 384], P('expert', 'dp'), may hold values from -0.3125 to 0.3125
Outputs:
- token_grad: bfloat16 [8192, 1536], P(('dp', 'expert'))
- prob_grad: float32 [8192, 8], P(('dp', 'expert'))
- grad_gate: bfloat16 [128, 1536, 384], P('expert', 'dp')
- grad_up: bfloat16 [128, 1536, 384], P('expert', 'dp')
- grad_down: bfloat16 [128, 1536, 384], P('expert', 'dp')
The draws below stay inside these ranges and needn't reach their ends.
Inputs may be any that keep to these rules, and one draw needn't show every extreme that they name: `routes`: within the tokens of one device no expert is named by more than 2 entries, a bound that some block reaches; a token names 8 different experts.
All inputs are finite; a program needn't handle non-finite values.
Results may differ from the reference program's by a relative error of at most 0.02.
Values may be sent and summed in bfloat16 or wider, within the bound.
No kernel may reach another device: no remote copies, remote signals or barrier semaphores. Data moves between devices by JAX's collectives and lax.ppermute only.
A program may use at most 64 MiB of HBM per device.

```python
import math
import jax
import jax.numpy as jnp
import numpy as np
from jax import lax

D = 1536
F = 384
TOP = 8
TOK_DEV = 16
EXPERTS = 128
MOST = 2
SLOTS = 256
TOKENS = 8192
N_DP = 4
N_EXPERT = 128


def steps_of(key, dims, split, smallest, largest):
    def one(dim, shards_of):
        draws = jax.random.uniform(jax.random.fold_in(jax.random.fold_in(key, 6), dim), (shards_of,), jnp.float32, smallest / len(split), largest / len(split))
        return jnp.repeat(jnp.exp(draws), dims[dim] // shards_of).reshape((-1,) + (1,) * (len(dims) - dim - 1))

    level = one(*split[0])
    for cut in split[1:]:
        level = level * one(*cut)
    return level


def deal_out(own_key, own, number, rows, amount, top, limit, lean):
    sequence = jax.random.permutation(own_key, amount)
    heavy_load, common = load_shares(amount, rows * top, limit, lean, True), load_shares(amount, rows * top, limit, lean, False)
    places = jnp.arange(amount)

    def named(tallies, turn):
        used = int((tallies > 0).sum())
        fixed = max(1, used // 4)
        moved = fixed + (places - fixed + turn * (used - fixed)) % max(1, amount - fixed)
        return jnp.zeros((amount,), jnp.int32).at[sequence[jnp.where(places < fixed, places, moved)]].set(jnp.asarray(tallies, jnp.int32))

    tallies = jnp.where(number % 4 == 0, named(heavy_load, number // 4), named(common, number - number // 4 - 1))
    mixed = jax.random.permutation(jax.random.fold_in(own, 3), amount)
    donor, sink = mixed[0:amount // 2 * 2:2], mixed[1:amount // 2 * 2:2]
    margin = jnp.minimum(tallies[donor] - 1, limit - tallies[sink]) // 2
    margin = jnp.where((donor == sequence[0]) | (sink == sequence[0]) | (tallies[sink] == 0), 0, jnp.maximum(margin, 0))
    moved = jax.random.randint(jax.random.fold_in(own, 4), (amount // 2,), 0, 1 << 20) % (margin + 1)
    tallies = tallies.at[donor].add(-moved).at[sink].add(moved)
    items = jnp.searchsorted(jnp.cumsum(tallies), jnp.arange(rows * top), side="right").astype(jnp.int32)
    table = items.reshape(top, rows).T
    table = table[jax.random.permutation(jax.random.fold_in(own, 1), rows)]
    turn = jax.random.randint(jax.random.fold_in(own, 2), (rows, 1), 0, top)
    return jnp.take_along_axis(table, (jnp.arange(top)[None, :] + turn) % top, axis=1)


def load_shares(count, total, most, slope, full):
    loads = [(1 << 20) // math.isqrt(standing ** slope) + 1 for standing in range(1, count + 1)]
    largest = most if full else min(most, max(-(-total // count), total * loads[0] // sum(loads)))
    least = 1 if total - largest >= count - 1 else 0
    counts, rest = [largest] + [least] * (count - 1), total - largest - least * (count - 1)
    while rest > 0:
        movable = [i for i in range(1, count) if counts[i] < largest] or [i for i in range(1, count) if counts[i] < most]
        mass, budget = sum([loads[i] for i in movable]), rest
        for i in movable:
            addition = min(most - counts[i], max(1, budget * loads[i] // mass), rest)
            counts[i] = counts[i] + addition
            rest = rest - addition
    return np.array(counts)


def gaussian(rng, dims, deviation, limit, shards=(), held_as=jnp.bfloat16):
    result = deviation * jax.random.normal(rng, dims, jnp.float32)
    if shards:
        result = result * steps_of(rng, dims, shards, -0.22, 0.18)
    return jnp.clip(result, -limit, limit).astype(held_as)


def setup_inputs(seed: int = 0) -> dict:
    key_of = jax.random.split(jax.random.key(seed), 8)
    out_grad = gaussian(key_of[0], (TOKENS, D), 0.25, 1.5, ((0, 512),))
    routes_keys = jax.random.split(jax.random.fold_in(key_of[1], 1), TOKENS // TOK_DEV)
    routes_turns = jax.random.permutation(jax.random.fold_in(key_of[1], 3), TOKENS // TOK_DEV)
    routes = jax.vmap(lambda own, number: deal_out(jax.random.fold_in(key_of[1], 2), own, number, TOK_DEV, EXPERTS, TOP, MOST, 2))(routes_keys, routes_turns).reshape((TOKENS, TOP))
    gate_probs = jnp.clip(jnp.exp(math.log(1.0) - 2.9957323 * jax.random.uniform(key_of[2], (TOKENS, TOP), jnp.float32) ** steps_of(key_of[2], (TOKENS, TOP), ((0, 512),), -0.2, 0.2)), 0.05, 1.0)
    saved_inputs = gaussian(key_of[3], (N_DP, EXPERTS, SLOTS, D), 1.0, 6.0, ((0, 4), (1, 128)))
    w_gate = gaussian(key_of[4], (EXPERTS, D, F), D ** -0.5, 0.15625, ((0, 128), (1, 4)))
    w_up = gaussian(key_of[5], (EXPERTS, D, F), D ** -0.5, 0.15625, ((0, 128), (1, 4)))
    w_down = gaussian(key_of[6], (EXPERTS, D, F), F ** -0.5, 0.3125, ((0, 128), (1, 4)))
    return dict(out_grad=out_grad, routes=routes, gate_probs=gate_probs, saved_inputs=saved_inputs, w_gate=w_gate, w_up=w_up, w_down=w_down)


def expert_grads(inputs_rows, grad_rows, prob, gate_w, up_w, down_w):
    pre_gate = jnp.dot(inputs_rows, gate_w, preferred_element_type=jnp.float32)
    pre_up = jnp.dot(inputs_rows, up_w, preferred_element_type=jnp.float32)
    sigma_g = jax.nn.sigmoid(pre_gate)
    activated = pre_gate * sigma_g
    hidden = activated * pre_up
    dh_raw = jnp.dot(grad_rows, down_w, preferred_element_type=jnp.float32)
    row_prob = jnp.sum(hidden * dh_raw, axis=1)
    scaled_hidden = (prob[:, None] * hidden).astype(jnp.bfloat16)
    dh_full = prob[:, None] * dh_raw
    d_up = (dh_full * activated).astype(jnp.bfloat16)
    d_gate = (dh_full * pre_up * sigma_g * (1.0 + pre_gate * (1.0 - sigma_g))).astype(jnp.bfloat16)
    row_grad = (jnp.dot(d_gate, gate_w.T, preferred_element_type=jnp.float32)
                + jnp.dot(d_up, up_w.T, preferred_element_type=jnp.float32)).astype(jnp.bfloat16)
    part_gate = jnp.dot(inputs_rows.T, d_gate, preferred_element_type=jnp.float32)
    part_up = jnp.dot(inputs_rows.T, d_up, preferred_element_type=jnp.float32)
    part_down = jnp.dot(grad_rows.T, scaled_hidden, preferred_element_type=jnp.float32)
    return row_grad, row_prob, part_gate, part_up, part_down


def slot_block(block):
    onehot = (block[:, None] == jnp.arange(EXPERTS, dtype=jnp.int32)[None, :]).astype(jnp.int32)
    running = jnp.cumsum(onehot, axis=0)
    return jnp.sum(onehot * (running - 1), axis=1).astype(jnp.int32)


def reference(out_grad, routes, gate_probs, saved_inputs, w_gate, w_up, w_down):
    pairs = TOK_DEV * TOP
    devices = N_DP * N_EXPERT
    blocks = routes.reshape(devices, pairs)
    slots = lax.map(slot_block, blocks).reshape(-1)
    pair_ids = jnp.arange(TOKENS * TOP, dtype=jnp.int32)
    device_of = pair_ids // pairs
    group_of = device_of // N_EXPERT
    source_of = device_of % N_EXPERT
    expert_of = routes.reshape(-1)
    table = jnp.full((N_DP, EXPERTS, SLOTS), TOKENS * TOP, dtype=jnp.int32)
    table = table.at[group_of, expert_of, source_of * MOST + slots].set(pair_ids)
    grad_padded = jnp.concatenate([out_grad, jnp.zeros((1, D), jnp.bfloat16)], axis=0)
    prob_padded = jnp.concatenate([gate_probs.reshape(-1), jnp.zeros((1,), jnp.float32)], axis=0)

    def per_expert(carry, expert):
        token_acc, prob_acc = carry
        sums_gate = jnp.zeros((D, F), jnp.float32)
        sums_up = jnp.zeros((D, F), jnp.float32)
        sums_down = jnp.zeros((D, F), jnp.float32)
        gate_w = w_gate[expert]
        up_w = w_up[expert]
        down_w = w_down[expert]
        for group in range(N_DP):
            index = table[group, expert]
            tokens_of = (index // TOP).astype(jnp.int32)
            grad_rows = grad_padded[tokens_of]
            prob = prob_padded[index]
            row_grad, row_prob, part_gate, part_up, part_down = expert_grads(
                saved_inputs[group, expert], grad_rows, prob, gate_w, up_w, down_w)
            token_acc = token_acc.at[tokens_of].add(row_grad.astype(jnp.float32))
            prob_acc = prob_acc.at[index].set(row_prob)
            sums_gate = sums_gate + part_gate.astype(jnp.bfloat16).astype(jnp.float32)
            sums_up = sums_up + part_up.astype(jnp.bfloat16).astype(jnp.float32)
            sums_down = sums_down + part_down.astype(jnp.bfloat16).astype(jnp.float32)
        outputs = (sums_gate.astype(jnp.bfloat16), sums_up.astype(jnp.bfloat16), sums_down.astype(jnp.bfloat16))
        return (token_acc, prob_acc), outputs

    start = (jnp.zeros((TOKENS + 1, D), jnp.float32), jnp.zeros((TOKENS * TOP + 1,), jnp.float32))
    (token_acc, prob_acc), grads = lax.scan(per_expert, start, jnp.arange(EXPERTS, dtype=jnp.int32))
    token_grad = token_acc[:TOKENS].astype(jnp.bfloat16)
    prob_grad = prob_acc[:TOKENS * TOP].reshape(TOKENS, TOP)
    return token_grad, prob_grad, grads[0], grads[1], grads[2]
```

```python
import jax
import jax.numpy as jnp
from jax import lax
from jax.experimental import pallas as pl
from jax.experimental.pallas import tpu as pltpu
from jax.sharding import PartitionSpec as P

TOP = 8
EXTRA = 128
BF = jnp.bfloat16
F32 = jnp.float32
PRE_COST = 10000 << 20
PARTS_COST = 10 << 20
ADD_COST = 4000 << 20
VMEM_LIMIT = 14 * 1024 * 1024


def dot(a, b):
    return jnp.dot(a, b, preferred_element_type=F32)


def dot_nt(a, b):
    return lax.dot_general(a, b, (((1,), (1,)), ((), ())), preferred_element_type=F32)


def dot_tn(a, b):
    return lax.dot_general(a, b, (((0,), (0,)), ((), ())), preferred_element_type=F32)


def call(body, outs, args, scratch=(), cost=(0, 0)):
    vmem = pl.BlockSpec(memory_space=pltpu.VMEM)
    return pl.pallas_call(
        body,
        out_shape=[jax.ShapeDtypeStruct(s, d) for s, d in outs],
        in_specs=[vmem] * len(args),
        out_specs=[vmem] * len(outs),
        scratch_shapes=list(scratch),
        compiler_params=pltpu.CompilerParams(vmem_limit_bytes=VMEM_LIMIT),
        cost_estimate=pl.CostEstimate(flops=cost[0], bytes_accessed=cost[1], transcendentals=0),
    )(*args)


def places(routes_t, slots, capacity):
    top, toks = routes_t.shape
    row = lax.broadcasted_iota(jnp.int32, (slots, toks), 0)
    expert = row // capacity
    hits = [routes_t[k : k + 1, :] == expert for k in range(top)]
    named = sum(h.astype(F32) for h in hits)
    before = (
        lax.broadcasted_iota(jnp.int32, (toks, toks), 0)
        < lax.broadcasted_iota(jnp.int32, (toks, toks), 1)
    ).astype(BF)
    rank = dot(named.astype(BF), before)
    mine = (named > 0.5) & (rank == (row - expert * capacity).astype(F32))
    return mine, hits


def build_kernel(routes_ref, probs_ref, grad_ref, out_ref):
    experts, capacity, width = out_ref.shape
    slots = experts * capacity
    mine, hits = places(routes_ref[...], slots, capacity)
    probs = probs_ref[...]
    weight = jnp.zeros(mine.shape, F32)
    for k, hit in enumerate(hits):
        weight = weight + jnp.where(hit, probs[k : k + 1, :], 0.0)
    weight = jnp.where(mine, weight, 0.0)
    high = weight.astype(BF)
    low = (weight - high.astype(F32)).astype(BF)
    grad = grad_ref[...]
    rows = (dot(high, grad) + dot(low, grad)).astype(BF)
    out_ref[...] = rows.reshape(experts, capacity, width)


def combine_kernel(routes_ref, probs_ref, back_ref, token_ref, prob_ref):
    experts, capacity, wide = back_ref.shape
    slots, width = experts * capacity, token_ref.shape[1]
    back = back_ref[...].reshape(slots, wide)
    mine, hits = places(routes_ref[...], slots, capacity)
    token_ref[...] = dot_tn(mine.astype(BF), back[:, :width]).astype(BF)
    value = jnp.sum(back[:, width:].astype(F32), axis=1, keepdims=True)
    probs = probs_ref[...]
    for k, hit in enumerate(hits):
        got = jnp.sum(jnp.where(hit & mine, value, 0.0), axis=0, keepdims=True)
        prob_ref[k : k + 1, :] = got / probs[k : k + 1, :]


def pack_kernel(a_ref, b_ref, c_ref, out_ref):
    n = a_ref.shape[0]
    out_ref[0:n, :] = a_ref[...]
    out_ref[n : 2 * n, :] = b_ref[...]
    out_ref[2 * n :, :] = c_ref[...]


def pieces(which, own_ref, right_ref, left_ref, first_ref, second_ref):
    n = own_ref.shape[0] // 3
    lo, hi, half = which * n, (which + 1) * n, first_ref.shape[0]
    if hi <= half:
        far = first_ref[lo:hi, :]
    elif lo >= half:
        far = second_ref[lo - half : hi - half, :]
    else:
        far = jnp.concatenate([first_ref[lo:half, :], second_ref[0 : hi - half, :]], axis=0)
    return ((0, own_ref[lo:hi, :]), (3, right_ref[lo:hi, :]), (1, left_ref[lo:hi, :]), (2, far))


def columns(offset, n):
    source = lax.rem(lax.axis_index("dp") + offset, 4)
    return pl.ds(pl.multiple_of(source * n, 128), n)


def contract(rows_ref, parts):
    total = None
    for offset, block in parts:
        term = dot(rows_ref[:, columns(offset, block.shape[0])], block)
        total = term if total is None else total + term
    return total


def pre_kernel(x_ref, own_ref, right_ref, left_ref, first_ref, second_ref, gate_ref, up_ref):
    weights = (own_ref, right_ref, left_ref, first_ref, second_ref)
    gate_ref[...] = contract(x_ref, pieces(0, *weights))
    up_ref[...] = contract(x_ref, pieces(1, *weights))


def middle_kernel(
    x_ref, rows_ref, gate_ref, up_ref, own_ref, right_ref, left_ref, first_ref, second_ref,
    row_ref, g_ref, dgate_ref, dup_ref, hidden_ref, far_a_ref, far_b_ref, row_scratch,
):
    weights = (own_ref, right_ref, left_ref, first_ref, second_ref)
    n = own_ref.shape[0] // 3
    width = x_ref.shape[1]
    half = far_a_ref.shape[0]
    g_ref[...] = rows_ref[...].reshape(g_ref.shape)
    dh = contract(g_ref, pieces(2, *weights))
    gate, up = gate_ref[...], up_ref[...]
    sig = jax.nn.sigmoid(gate)
    act = gate * sig
    hidden = act * up
    row_prob = jnp.sum(hidden * dh, axis=1, keepdims=True)
    d_up = (dh * act).astype(BF)
    d_gate = (dh * up * sig * (1.0 + gate * (1.0 - sig))).astype(BF)
    hidden = hidden.astype(BF)
    dgate_ref[...] = d_gate
    dup_ref[...] = d_up
    hidden_ref[...] = hidden
    far = columns(2, n)
    far_a_ref[0:n, :] = dot_tn(x_ref[:, far], d_gate).astype(BF)
    part_up = dot_tn(x_ref[:, far], d_up).astype(BF)
    far_a_ref[n:half, :] = part_up[0 : half - n, :]
    far_b_ref[0 : 2 * n - half, :] = part_up[half - n :, :]
    far_b_ref[2 * n - half :, :] = dot_tn(g_ref[:, far], hidden).astype(BF)
    for (offset, g_block), (_, u_block) in zip(pieces(0, *weights), pieces(1, *weights)):
        row_scratch[:, columns(offset, n)] = (dot_nt(d_gate, g_block) + dot_nt(d_up, u_block)).astype(BF)
    lane = lax.broadcasted_iota(jnp.int32, (x_ref.shape[0], EXTRA), 1)
    high = row_prob.astype(BF).astype(F32)
    row_scratch[:, width:] = jnp.where(
        lane == 0, high, jnp.where(lane == 1, row_prob - high, 0.0)
    ).astype(BF)
    row_ref[...] = row_scratch[...].reshape(row_ref.shape)


def parts_kernel(x_ref, g_ref, dgate_ref, dup_ref, hidden_ref, own_ref, right_ref, left_ref):
    n = x_ref.shape[1] // 4
    for offset, out in ((1, right_ref), (3, left_ref), (0, own_ref)):
        cols = columns(offset, n)
        out[0:n, :] = dot_tn(x_ref[:, cols], dgate_ref[...]).astype(BF)
        out[n : 2 * n, :] = dot_tn(x_ref[:, cols], dup_ref[...]).astype(BF)
        out[2 * n :, :] = dot_tn(g_ref[:, cols], hidden_ref[...]).astype(BF)


def add_kernel(right_ref, left_ref, from_left_ref, from_right_ref, to_right_ref, to_left_ref):
    half = from_left_ref.shape[0]
    to_right_ref[0:half, :] = (
        right_ref[0:half, :].astype(F32) + from_left_ref[...].astype(F32)
    ).astype(BF)
    to_right_ref[half:, :] = right_ref[half:, :]
    to_left_ref[0:half, :] = left_ref[0:half, :]
    to_left_ref[half:, :] = (
        left_ref[half:, :].astype(F32) + from_right_ref[...].astype(F32)
    ).astype(BF)


def sum_kernel(own_ref, a_ref, b_ref, gate_ref, up_ref, down_ref):
    n = gate_ref.shape[0]
    for i, out in enumerate((gate_ref, up_ref, down_ref)):
        at = slice(i * n, (i + 1) * n)
        out[...] = (
            own_ref[at, :].astype(F32) + a_ref[at, :].astype(F32) + b_ref[at, :].astype(F32)
        ).astype(BF)


def shift(value, by):
    return lax.ppermute(value, "dp", [(i, (i + by) % 4) for i in range(4)])


def shards(out_grad, routes, gate_probs, saved_inputs, w_gate, w_up, w_down):
    toks, width = out_grad.shape
    experts = lax.axis_size("expert")
    slots = saved_inputs.shape[2]
    capacity = slots // experts
    n, f = w_gate.shape[1], w_gate.shape[2]
    half = 3 * n // 2
    x = saved_inputs[0, 0]
    routes_t, probs_t = routes.T, gate_probs.T

    (own,) = call(pack_kernel, [((3 * n, f), BF)], (w_gate[0], w_up[0], w_down[0]), cost=(0, 12 * n * f))
    right = shift(own, 1)
    left = shift(own, -1)
    (send,) = call(
        build_kernel,
        [((experts, capacity, width), BF)],
        (routes_t, probs_t, out_grad),
        cost=(0, 2 * slots * width),
    )
    rows = lax.all_to_all(send, "expert", split_axis=0, concat_axis=0, tiled=True)
    first = shift(right[:half], 1)
    second = shift(left[half:], -1)
    weights = (own, right, left, first, second)
    pre_gate, pre_up = call(
        pre_kernel, [((slots, f), F32)] * 2, (x, *weights), cost=(PRE_COST, 0)
    )
    row_grad, g, d_gate, d_up, hidden, far_a, far_b = call(
        middle_kernel,
        [((experts, capacity, width + EXTRA), BF), ((slots, width), BF)]
        + [((slots, f), BF)] * 3
        + [((half, f), BF)] * 2,
        (x, rows, pre_gate, pre_up, *weights),
        scratch=[pltpu.VMEM((slots, width + EXTRA), BF)],
        cost=(8 * slots * width * f, 8 << 20),
    )
    from_left = shift(far_a, 1)
    from_right = shift(far_b, -1)
    back = lax.all_to_all(row_grad, "expert", split_axis=0, concat_axis=0, tiled=True)
    mine, to_right, to_left = call(
        parts_kernel,
        [((3 * n, f), BF)] * 3,
        (x, g, d_gate, d_up, hidden),
        cost=(PARTS_COST, 0),
    )
    to_right, to_left = call(
        add_kernel, [((3 * n, f), BF)] * 2, (to_right, to_left, from_left, from_right), cost=(ADD_COST, 0)
    )
    a = shift(to_right, 1)
    b = shift(to_left, -1)
    grads = call(sum_kernel, [((n, f), BF)] * 3, (mine, a, b), cost=(ADD_COST, 0))
    token_grad, prob_t = call(
        combine_kernel,
        [((toks, width), BF), (probs_t.shape, F32)],
        (routes_t, probs_t, back),
        cost=(0, 1 << 20),
    )
    return (token_grad, prob_t.T, grads[0][None], grads[1][None], grads[2][None])


def solution(mesh):
    return jax.shard_map(
        shards,
        mesh=mesh,
        in_specs=(
            P(("dp", "expert"), None),
            P(("dp", "expert"), None),
            P(("dp", "expert"), None),
            P("dp", "expert", None, None),
            P("expert", "dp", None),
            P("expert", "dp", None),
            P("expert", "dp", None),
        ),
        out_specs=(
            P(("dp", "expert"), None),
            P(("dp", "expert"), None),
            P("expert", "dp", None),
            P("expert", "dp", None),
            P("expert", "dp", None),
        ),
        check_vma=False,
    )
```

```python
import jax
import jax.numpy as jnp
from jax import lax
from jax.experimental import pallas as pl
from jax.experimental.pallas import tpu as pltpu
from jax.sharding import PartitionSpec as P

TOP = 8
EXTRA = 128
BF = jnp.bfloat16
F32 = jnp.float32
PRE_COST = 12000 << 20
SUM_COST = 12000 << 20


def dot(a, b):
    return jnp.dot(a, b, preferred_element_type=F32)


def dot_nt(a, b):
    return lax.dot_general(a, b, (((1,), (1,)), ((), ())), preferred_element_type=F32)


def dot_tn(a, b):
    return lax.dot_general(a, b, (((0,), (0,)), ((), ())), preferred_element_type=F32)


def call(body, outs, args, scratch=(), flops=0, where=pltpu.HBM, mib=61):
    spec = pl.BlockSpec(memory_space=where)
    return pl.pallas_call(
        body,
        out_shape=[jax.ShapeDtypeStruct(s, d) for s, d in outs],
        in_specs=[spec] * len(args),
        out_specs=[spec] * len(outs),
        scratch_shapes=list(scratch),
        compiler_params=pltpu.CompilerParams(vmem_limit_bytes=mib * 1024 * 1024),
        cost_estimate=pl.CostEstimate(flops=flops, bytes_accessed=0, transcendentals=0),
    )(*args)


def start(copies, sems):
    made = [pltpu.make_async_copy(a, b, sems.at[i]) for i, (a, b) in enumerate(copies)]
    for c in made:
        c.start()
    return made


def finish(copies):
    for c in copies:
        c.wait()


def places(routes_t, slots, capacity):
    top, toks = routes_t.shape
    row = lax.broadcasted_iota(jnp.int32, (slots, toks), 0)
    expert = row // capacity
    hits = [routes_t[k : k + 1, :] == expert for k in range(top)]
    named = sum(h.astype(F32) for h in hits)
    before = (
        lax.broadcasted_iota(jnp.int32, (toks, toks), 0)
        < lax.broadcasted_iota(jnp.int32, (toks, toks), 1)
    ).astype(BF)
    rank = dot(named.astype(BF), before)
    mine = (named > 0.5) & (rank == (row - expert * capacity).astype(F32))
    return mine, hits


def build_kernel(routes_ref, probs_ref, grad_ref, out_ref):
    experts, capacity, width = out_ref.shape
    slots = experts * capacity
    mine, hits = places(routes_ref[...], slots, capacity)
    probs = probs_ref[...]
    weight = jnp.zeros(mine.shape, F32)
    for k, hit in enumerate(hits):
        weight = weight + jnp.where(hit, probs[k : k + 1, :], 0.0)
    weight = jnp.where(mine, weight, 0.0)
    high = weight.astype(BF)
    low = (weight - high.astype(F32)).astype(BF)
    grad = grad_ref[...]
    rows = (dot(high, grad) + dot(low, grad)).astype(BF)
    out_ref[...] = rows.reshape(experts, capacity, width)


def combine_kernel(routes_ref, probs_ref, back_ref, token_ref, prob_ref):
    experts, capacity, wide = back_ref.shape
    slots, width = experts * capacity, token_ref.shape[1]
    back = back_ref[...].reshape(slots, wide)
    mine, hits = places(routes_ref[...], slots, capacity)
    token_ref[...] = dot_tn(mine.astype(BF), back[:, :width]).astype(BF)
    value = jnp.sum(back[:, width:].astype(F32), axis=1, keepdims=True)
    probs = probs_ref[...]
    for k, hit in enumerate(hits):
        got = jnp.sum(jnp.where(hit & mine, value, 0.0), axis=0, keepdims=True)
        prob_ref[k : k + 1, :] = got / probs[k : k + 1, :]


def pack_kernel(a_ref, b_ref, c_ref, out_hbm, out_ref, sems):
    n = a_ref.shape[0]
    blocks = [pl.ds(i * n, n) for i in range(3)]
    copies = start([(r, out_ref.at[at, :]) for r, at in zip((a_ref, b_ref, c_ref), blocks)], sems)
    out = []
    for i, at in enumerate(blocks):
        copies[i].wait()
        out += start([(out_ref.at[at, :], out_hbm.at[at, :])], sems.at[pl.ds(3 + i, 1)])
    finish(out)


def span(offset, n):
    source = lax.rem(lax.axis_index("dp") + offset, 4)
    return pl.ds(pl.multiple_of(source * n, 128), n)


def pre_kernel(x_hbm, own, far, acc_hbm, x_ref, w_ref, acc_ref, sems):
    n, f = own.shape[0] // 3, own.shape[1]
    moves = []
    for i, (offset, block) in enumerate(((0, own), (2, far))):
        at = pl.ds(i * n, n)
        moves.append((x_hbm.at[:, span(offset, n)], x_ref.at[:, at]))
        moves.append((block.at[pl.ds(0, n), :], w_ref.at[at, pl.ds(0, f)]))
        moves.append((block.at[pl.ds(n, n), :], w_ref.at[at, pl.ds(f, f)]))
    finish(start(moves, sems))
    acc_ref[...] = dot(x_ref[...], w_ref[...])
    finish(start([(acc_ref, acc_hbm)], sems))


def middle_kernel(
    x_hbm, rows_hbm, acc_hbm, own, right, left, far,
    back_hbm, to_own, to_right, to_left, to_far,
    x_ref, rows_ref, acc_ref, w_ref, wd_ref, g_ref, row_ref, back_ref, part_ref, sems,
):
    width, n, f = x_ref.shape[1], x_ref.shape[1] // 4, wd_ref.shape[1]
    moves = [(rows_hbm, rows_ref), (x_hbm, x_ref), (acc_hbm, acc_ref)]
    for offset, block in ((3, right), (1, left), (0, own), (2, far)):
        at = span(offset, n)
        moves.append((block.at[pl.ds(0, n), :], w_ref.at[at, pl.ds(0, f)]))
        moves.append((block.at[pl.ds(n, n), :], w_ref.at[at, pl.ds(f, f)]))
        moves.append((block.at[pl.ds(2 * n, n), :], wd_ref.at[at, :]))
    copies = start(moves, sems)
    finish(copies[0:1])
    g_ref[...] = rows_ref[...].reshape(g_ref.shape)
    finish(copies[1:])
    pre = acc_ref[...]
    for offset in (3, 1):
        pre = pre + dot(x_ref[:, span(offset, n)], w_ref[span(offset, n), :])
    dh = dot(g_ref[...], wd_ref[...])
    gate, up = pre[:, :f], pre[:, f:]
    sig = jax.nn.sigmoid(gate)
    act = gate * sig
    hidden = act * up
    row_prob = jnp.sum(hidden * dh, axis=1, keepdims=True)
    d_up = (dh * act).astype(BF)
    d_gate = (dh * up * sig * (1.0 + gate * (1.0 - sig))).astype(BF)
    hidden = hidden.astype(BF)
    both = jnp.concatenate([d_gate, d_up], axis=1)
    out = []
    for k, (offset, to) in enumerate(((2, to_far), (1, to_right), (3, to_left), (0, to_own))):
        cols = span(offset, n)
        part = dot_tn(x_ref[:, cols], both).astype(BF)
        part_ref[k, 0:n, :] = part[:, :f]
        part_ref[k, n : 2 * n, :] = part[:, f:]
        part_ref[k, 2 * n :, :] = dot_tn(g_ref[:, cols], hidden).astype(BF)
        out += start([(part_ref.at[k], to)], sems.at[pl.ds(15 + k, 1)])
    for i in range(4):
        at = slice(i * n, (i + 1) * n)
        row_ref[:, at] = dot_nt(both, w_ref[at, :]).astype(BF)
    lane = lax.broadcasted_iota(jnp.int32, (x_ref.shape[0], EXTRA), 1)
    high = row_prob.astype(BF).astype(F32)
    row_ref[:, width:] = jnp.where(
        lane == 0, high, jnp.where(lane == 1, row_prob - high, 0.0)
    ).astype(BF)
    back_ref[...] = row_ref[...].reshape(back_ref.shape)
    out += start([(back_ref, back_hbm)], sems.at[pl.ds(19, 1)])
    finish(out)


def first_sum_kernel(own, far, sum_hbm, in_ref, sum_ref, sems):
    finish(start([(own, in_ref.at[0]), (far, in_ref.at[1])], sems))
    sum_ref[...] = in_ref[0].astype(F32) + in_ref[1].astype(F32)
    finish(start([(sum_ref, sum_hbm)], sems))


def last_sum_kernel(sum_hbm, a, b, gate_hbm, up_hbm, down_hbm, sum_ref, in_ref, out_ref, sems):
    n = gate_hbm.shape[0]
    blocks = [pl.ds(i * n, n) for i in range(3)]
    moves = []
    for at in blocks:
        moves += [(sum_hbm.at[at, :], sum_ref.at[at, :])]
        moves += [(r.at[at, :], in_ref.at[k, at, :]) for k, r in enumerate((a, b))]
    copies = start(moves, sems)
    out = []
    for i, hbm in enumerate((gate_hbm, up_hbm, down_hbm)):
        finish(copies[3 * i : 3 * i + 3])
        at = blocks[i]
        out_ref[at, :] = (
            sum_ref[at, :] + in_ref[0, at, :].astype(F32) + in_ref[1, at, :].astype(F32)
        ).astype(BF)
        out += start([(out_ref.at[at, :], hbm)], sems.at[pl.ds(9 + i, 1)])
    finish(out)


def shift(value, by):
    return lax.ppermute(value, "dp", [(i, (i + by) % 4) for i in range(4)])


def shards(out_grad, routes, gate_probs, saved_inputs, w_gate, w_up, w_down):
    toks, width = out_grad.shape
    experts = lax.axis_size("expert")
    slots = saved_inputs.shape[2]
    capacity = slots // experts
    n, f = w_gate.shape[1], w_gate.shape[2]
    x = saved_inputs[0, 0]
    routes_t, probs_t = routes.T, gate_probs.T
    dma = pltpu.SemaphoreType.DMA
    block = ((3 * n, f), BF)
    row_block = (experts, capacity, width + EXTRA)

    (own,) = call(
        pack_kernel, [block], (w_gate[0], w_up[0], w_down[0]), [pltpu.VMEM(*block), dma((6,))]
    )
    far = shift(own, 2)
    (send,) = call(
        build_kernel,
        [((experts, capacity, width), BF)],
        (routes_t, probs_t, out_grad),
        where=pltpu.VMEM,
        mib=16,
    )
    rows = lax.all_to_all(send, "expert", split_axis=0, concat_axis=0, tiled=True)
    right = shift(own, 1)
    left = shift(own, -1)
    (acc,) = call(
        pre_kernel,
        [((slots, 2 * f), F32)],
        (x, own, far),
        [
            pltpu.VMEM((slots, 2 * n), BF),
            pltpu.VMEM((2 * n, 2 * f), BF),
            pltpu.VMEM((slots, 2 * f), F32),
            dma((6,)),
        ],
        flops=PRE_COST,
    )
    row_grad, to_own, to_right, to_left, to_far = call(
        middle_kernel,
        [(row_block, BF)] + [block] * 4,
        (x, rows, acc, own, right, left, far),
        [
            pltpu.VMEM((slots, width), BF),
            pltpu.VMEM((experts, capacity, width), BF),
            pltpu.VMEM((slots, 2 * f), F32),
            pltpu.VMEM((width, 2 * f), BF),
            pltpu.VMEM((width, f), BF),
            pltpu.VMEM((slots, width), BF),
            pltpu.VMEM((slots, width + EXTRA), BF),
            pltpu.VMEM(row_block, BF),
            pltpu.VMEM((4, 3 * n, f), BF),
            dma((20,)),
        ],
        mib=60,
    )
    from_far = shift(to_far, 2)
    back = lax.all_to_all(row_grad, "expert", split_axis=0, concat_axis=0, tiled=True)
    from_left = shift(to_right, 1)
    from_right = shift(to_left, -1)
    (total,) = call(
        first_sum_kernel,
        [((3 * n, f), F32)],
        (to_own, from_far),
        [pltpu.VMEM((2, 3 * n, f), BF), pltpu.VMEM((3 * n, f), F32), dma((2,))],
        flops=SUM_COST,
        mib=30,
    )
    grads = call(
        last_sum_kernel,
        [((n, f), BF)] * 3,
        (total, from_left, from_right),
        [
            pltpu.VMEM((3 * n, f), F32),
            pltpu.VMEM((2, 3 * n, f), BF),
            pltpu.VMEM((3 * n, f), BF),
            dma((12,)),
        ],
        mib=30,
    )
    token_grad, prob_t = call(
        combine_kernel,
        [((toks, width), BF), (probs_t.shape, F32)],
        (routes_t, probs_t, back),
        where=pltpu.VMEM,
        mib=16,
    )
    return (token_grad, prob_t.T, grads[0][None], grads[1][None], grads[2][None])


def solution(mesh):
    return jax.shard_map(
        shards,
        mesh=mesh,
        in_specs=(
            P(("dp", "expert"), None),
            P(("dp", "expert"), None),
            P(("dp", "expert"), None),
            P("dp", "expert", None, None),
            P("expert", "dp", None),
            P("expert", "dp", None),
            P("expert", "dp", None),
        ),
        out_specs=(
            P(("dp", "expert"), None),
            P(("dp", "expert"), None),
            P("expert", "dp", None),
            P("expert", "dp", None),
            P("expert", "dp", None),
        ),
        check_vma=False,
    )
```

```python
import jax
import jax.numpy as jnp
from jax import lax
from jax.experimental import pallas as pl
from jax.experimental.pallas import tpu as pltpu
from jax.sharding import PartitionSpec as P

TOP = 8
EXTRA = 128
BF = jnp.bfloat16
F32 = jnp.float32
PRE_COST = 12000 << 20
SUM_COST = 12000 << 20
MID_MIB = 52
LAST_MIB = 20


def dot(a, b):
    return jnp.dot(a, b, preferred_element_type=F32)


def dot_nt(a, b):
    return lax.dot_general(a, b, (((1,), (1,)), ((), ())), preferred_element_type=F32)


def dot_tn(a, b):
    return lax.dot_general(a, b, (((0,), (0,)), ((), ())), preferred_element_type=F32)


def call(body, outs, args, scratch=(), flops=0, where=pltpu.HBM, mib=61):
    spaces = where if isinstance(where, tuple) else (where,) * (len(args) + len(outs))
    specs = [pl.BlockSpec(memory_space=space) for space in spaces]
    return pl.pallas_call(
        body,
        out_shape=[jax.ShapeDtypeStruct(s, d) for s, d in outs],
        in_specs=specs[: len(args)],
        out_specs=specs[len(args) :],
        scratch_shapes=list(scratch),
        compiler_params=pltpu.CompilerParams(vmem_limit_bytes=mib * 1024 * 1024),
        cost_estimate=pl.CostEstimate(flops=flops, bytes_accessed=0, transcendentals=0),
    )(*args)


def start(copies, sems):
    made = [pltpu.make_async_copy(a, b, sems.at[i]) for i, (a, b) in enumerate(copies)]
    for c in made:
        c.start()
    return made


def finish(copies):
    for c in copies:
        c.wait()


def places(routes_t, slots, capacity):
    top, toks = routes_t.shape
    row = lax.broadcasted_iota(jnp.int32, (slots, toks), 0)
    expert = row // capacity
    hits = [routes_t[k : k + 1, :] == expert for k in range(top)]
    named = sum(h.astype(F32) for h in hits)
    before = (
        lax.broadcasted_iota(jnp.int32, (toks, toks), 0)
        < lax.broadcasted_iota(jnp.int32, (toks, toks), 1)
    ).astype(BF)
    rank = dot(named.astype(BF), before)
    mine = (named > 0.5) & (rank == (row - expert * capacity).astype(F32))
    return mine, hits


def combine_kernel(routes_ref, probs_ref, back_ref, token_ref, prob_ref):
    experts, capacity, wide = back_ref.shape
    slots, width = experts * capacity, token_ref.shape[1]
    mine, hits = places(routes_ref[...], slots, capacity)
    picks = mine.astype(BF)
    n = width // 4
    for i in range(4):
        cols = slice(i * n, (i + 1) * n)
        token_ref[:, cols] = dot_tn(picks, back_ref[:, :, cols].reshape(slots, n)).astype(BF)
    extra = back_ref[:, :, width:].reshape(slots, wide - width)
    value = jnp.sum(extra.astype(F32), axis=1, keepdims=True)
    probs = probs_ref[...]
    for k, hit in enumerate(hits):
        got = jnp.sum(jnp.where(hit & mine, value, 0.0), axis=0, keepdims=True)
        prob_ref[k : k + 1, :] = got / probs[k : k + 1, :]


def open_kernel(
    a_hbm, b_hbm, c_hbm, routes_hbm, probs_hbm, grad_hbm, own_hbm, send_hbm,
    own_ref, routes_ref, probs_ref, grad_ref, send_ref, sems,
):
    n = a_hbm.shape[0]
    experts, capacity, width = send_ref.shape
    shard = start(
        [(r, own_ref.at[pl.ds(i * n, n), :]) for i, r in enumerate((a_hbm, b_hbm, c_hbm))], sems
    )
    small = start(
        [(routes_hbm, routes_ref), (probs_hbm, probs_ref), (grad_hbm, grad_ref)],
        sems.at[pl.ds(3, 3)],
    )
    finish(shard)
    out = start([(own_ref, own_hbm)], sems.at[pl.ds(6, 1)])
    finish(small)
    mine, hits = places(routes_ref[...], experts * capacity, capacity)
    probs = probs_ref[...]
    weight = jnp.zeros(mine.shape, F32)
    for k, hit in enumerate(hits):
        weight = weight + jnp.where(hit, probs[k : k + 1, :], 0.0)
    weight = jnp.where(mine, weight, 0.0)
    high = weight.astype(BF)
    low = (weight - high.astype(F32)).astype(BF)
    for i in range(4):
        cols = slice(i * n, (i + 1) * n)
        rows = dot(high, grad_ref[:, cols]) + dot(low, grad_ref[:, cols])
        send_ref[:, :, cols] = rows.astype(BF).reshape(experts, capacity, n)
    finish(out + start([(send_ref, send_hbm)], sems.at[pl.ds(7, 1)]))


def span(offset, n):
    source = lax.rem(lax.axis_index("dp") + offset, 4)
    return pl.ds(pl.multiple_of(source * n, 128), n)


def pre_kernel(x_hbm, own, far, acc_hbm, x_ref, w_ref, acc_ref, sems):
    n, f = own.shape[0] // 3, own.shape[1]
    moves = []
    for i, (offset, block) in enumerate(((0, own), (2, far))):
        at = pl.ds(i * n, n)
        moves.append((x_hbm.at[:, span(offset, n)], x_ref.at[:, at]))
        moves.append((block.at[pl.ds(0, n), :], w_ref.at[at, pl.ds(0, f)]))
        moves.append((block.at[pl.ds(n, n), :], w_ref.at[at, pl.ds(f, f)]))
    finish(start(moves, sems))
    acc_ref[...] = dot(x_ref[...], w_ref[...])
    finish(start([(acc_ref, acc_hbm)], sems))


def middle_kernel(
    x_ref, rows_ref, acc_hbm, own, right, left, far,
    back_hbm, to_own, to_right, to_left, to_far,
    acc_ref, w_ref, wd_ref, g_ref, back_ref, part_ref, sems,
):
    width, n, f = x_ref.shape[1], x_ref.shape[1] // 4, wd_ref.shape[1]
    blocks = ((3, right), (1, left), (0, own), (2, far))
    moves = [(b.at[pl.ds(2 * n, n), :], wd_ref.at[span(i, n), :]) for i, b in blocks]
    moves += [(acc_hbm, acc_ref)]
    for i, b in blocks:
        moves += [(b.at[pl.ds(k * n, n), :], w_ref.at[span(i, n), pl.ds(k * f, f)]) for k in (0, 1)]
    copies = start(moves, sems)
    slots, shape = x_ref.shape[0], rows_ref.shape
    finish(copies[0:4])
    dh = None
    for i in range(4):
        cols = slice(i * n, (i + 1) * n)
        rows = rows_ref[:, :, cols].reshape(slots, n)
        g_ref[:, cols] = rows
        term = dot(rows, wd_ref[cols, :])
        dh = term if dh is None else dh + term
    finish(copies[4:9])
    pre = acc_ref[...]
    for offset in (3, 1):
        pre = pre + dot(x_ref[:, span(offset, n)], w_ref[span(offset, n), :])
    gate, up = pre[:, :f], pre[:, f:]
    sig = jax.nn.sigmoid(gate)
    act = gate * sig
    hidden = act * up
    row_prob = jnp.sum(hidden * dh, axis=1, keepdims=True)
    d_up = (dh * act).astype(BF)
    d_gate = (dh * up * sig * (1.0 + gate * (1.0 - sig))).astype(BF)
    hidden = hidden.astype(BF)
    both = jnp.concatenate([d_gate, d_up], axis=1)
    out = []
    for k, (offset, to) in enumerate(((2, to_far), (1, to_right), (3, to_left), (0, to_own))):
        cols = span(offset, n)
        part = dot_tn(x_ref[:, cols], both).astype(BF)
        part_ref[k, 0:n, :] = part[:, :f]
        part_ref[k, n : 2 * n, :] = part[:, f:]
        part_ref[k, 2 * n :, :] = dot_tn(g_ref[:, cols], hidden).astype(BF)
        out += start([(part_ref.at[k], to)], sems.at[pl.ds(15 + k, 1)])
    finish(copies[9:13])
    for i in range(4):
        at = slice(i * n, (i + 1) * n)
        back_ref[:, :, at] = dot_nt(both, w_ref[at, :]).astype(BF).reshape(*shape[:2], n)
    lane = lax.broadcasted_iota(jnp.int32, (x_ref.shape[0], EXTRA), 1)
    high = row_prob.astype(BF).astype(F32)
    extra = jnp.where(lane == 0, high, jnp.where(lane == 1, row_prob - high, 0.0)).astype(BF)
    back_ref[:, :, width:] = extra.reshape(*shape[:2], EXTRA)
    out += start([(back_ref, back_hbm)], sems.at[pl.ds(19, 1)])
    finish(out)


def first_sum_kernel(own, far, sum_hbm, in_ref, sum_ref, sems):
    finish(start([(own, in_ref.at[0]), (far, in_ref.at[1])], sems))
    sum_ref[...] = in_ref[0].astype(F32) + in_ref[1].astype(F32)
    finish(start([(sum_ref, sum_hbm)], sems))


def last_sum_kernel(sum_ref, a_ref, b_ref, gate_hbm, up_hbm, down_hbm, out_ref, sems):
    n = gate_hbm.shape[0]
    out = []
    for i, hbm in enumerate((gate_hbm, up_hbm, down_hbm)):
        at = pl.ds(i * n, n)
        out_ref[at, :] = (
            sum_ref[at, :] + a_ref[at, :].astype(F32) + b_ref[at, :].astype(F32)
        ).astype(BF)
        out += start([(out_ref.at[at, :], hbm)], sems.at[pl.ds(i, 1)])
    finish(out)


def shift(value, by):
    return lax.ppermute(value, "dp", [(i, (i + by) % 4) for i in range(4)])


def shards(out_grad, routes, gate_probs, saved_inputs, w_gate, w_up, w_down):
    toks, width = out_grad.shape
    experts = lax.axis_size("expert")
    slots = saved_inputs.shape[2]
    capacity = slots // experts
    n, f = w_gate.shape[1], w_gate.shape[2]
    x = saved_inputs[0, 0]
    routes_t, probs_t = routes.T, gate_probs.T
    dma = pltpu.SemaphoreType.DMA
    block = ((3 * n, f), BF)
    row_block = (experts, capacity, width + EXTRA)

    own, send = call(
        open_kernel,
        [block, ((experts, capacity, width), BF)],
        (w_gate[0], w_up[0], w_down[0], routes_t, probs_t, out_grad),
        [
            pltpu.VMEM(*block),
            pltpu.VMEM(routes_t.shape, jnp.int32),
            pltpu.VMEM(probs_t.shape, F32),
            pltpu.VMEM(out_grad.shape, BF),
            pltpu.VMEM((experts, capacity, width), BF),
            dma((8,)),
        ],
    )
    far = shift(own, 2)
    rows = lax.all_to_all(send, "expert", split_axis=0, concat_axis=0, tiled=True)
    right = shift(own, 1)
    left = shift(own, -1)
    (acc,) = call(
        pre_kernel,
        [((slots, 2 * f), F32)],
        (x, own, far),
        [
            pltpu.VMEM((slots, 2 * n), BF),
            pltpu.VMEM((2 * n, 2 * f), BF),
            pltpu.VMEM((slots, 2 * f), F32),
            dma((6,)),
        ],
        flops=PRE_COST,
    )
    row_grad, to_own, to_right, to_left, to_far = call(
        middle_kernel,
        [(row_block, BF)] + [block] * 4,
        (x, rows, acc, own, right, left, far),
        [
            pltpu.VMEM((slots, 2 * f), F32),
            pltpu.VMEM((width, 2 * f), BF),
            pltpu.VMEM((width, f), BF),
            pltpu.VMEM((slots, width), BF),
            pltpu.VMEM(row_block, BF),
            pltpu.VMEM((4, 3 * n, f), BF),
            dma((20,)),
        ],
        where=(pltpu.VMEM,) * 2 + (pltpu.HBM,) * 10,
        mib=MID_MIB,
    )
    from_far = shift(to_far, 2)
    back = lax.all_to_all(row_grad, "expert", split_axis=0, concat_axis=0, tiled=True)
    from_left = shift(to_right, 1)
    from_right = shift(to_left, -1)
    (total,) = call(
        first_sum_kernel,
        [((3 * n, f), F32)],
        (to_own, from_far),
        [pltpu.VMEM((2, 3 * n, f), BF), pltpu.VMEM((3 * n, f), F32), dma((2,))],
        flops=SUM_COST,
        mib=30,
    )
    grads = call(
        last_sum_kernel,
        [((n, f), BF)] * 3,
        (total, from_left, from_right),
        [pltpu.VMEM((3 * n, f), BF), dma((3,))],
        where=(pltpu.VMEM,) * 3 + (pltpu.HBM,) * 3,
        mib=LAST_MIB,
    )
    token_grad, prob_t = call(
        combine_kernel,
        [((toks, width), BF), (probs_t.shape, F32)],
        (routes_t, probs_t, back),
        where=pltpu.VMEM,
        mib=16,
    )
    return (token_grad, prob_t.T, grads[0][None], grads[1][None], grads[2][None])


def solution(mesh):
    return jax.shard_map(
        shards,
        mesh=mesh,
        in_specs=(
            P(("dp", "expert"), None),
            P(("dp", "expert"), None),
            P(("dp", "expert"), None),
            P("dp", "expert", None, None),
            P("expert", "dp", None),
            P("expert", "dp", None),
            P("expert", "dp", None),
        ),
        out_specs=(
            P(("dp", "expert"), None),
            P(("dp", "expert"), None),
            P("expert", "dp", None),
            P("expert", "dp", None),
            P("expert", "dp", None),
        ),
        check_vma=False,
    )
```

```python
import jax
import jax.numpy as jnp
from jax import lax
from jax.experimental import pallas as pl
from jax.experimental.pallas import tpu as pltpu
from jax.sharding import PartitionSpec as P

TOP = 8
EXTRA = 128
BF = jnp.bfloat16
F32 = jnp.float32
PRE_COST = 9000 << 20
SUM_COST = 12000 << 20
MID_MIB = 50
EARLY_MIB = 50
EARLY_COST = 3000 << 20
LAST_MIB = 20


def dot(a, b):
    return jnp.dot(a, b, preferred_element_type=F32)


def dot_nt(a, b):
    return lax.dot_general(a, b, (((1,), (1,)), ((), ())), preferred_element_type=F32)


def dot_tn(a, b):
    return lax.dot_general(a, b, (((0,), (0,)), ((), ())), preferred_element_type=F32)


def call(body, outs, args, scratch=(), flops=0, where=pltpu.HBM, mib=61):
    spaces = where if isinstance(where, tuple) else (where,) * (len(args) + len(outs))
    specs = [pl.BlockSpec(memory_space=space) for space in spaces]
    return pl.pallas_call(
        body,
        out_shape=[jax.ShapeDtypeStruct(s, d) for s, d in outs],
        in_specs=specs[: len(args)],
        out_specs=specs[len(args) :],
        scratch_shapes=list(scratch),
        compiler_params=pltpu.CompilerParams(vmem_limit_bytes=mib * 1024 * 1024),
        cost_estimate=pl.CostEstimate(flops=flops, bytes_accessed=0, transcendentals=0),
    )(*args)


def start(copies, sems):
    made = [pltpu.make_async_copy(a, b, sems.at[i]) for i, (a, b) in enumerate(copies)]
    for c in made:
        c.start()
    return made


def finish(copies):
    for c in copies:
        c.wait()


def places(routes_t, slots, capacity):
    top, toks = routes_t.shape
    row = lax.broadcasted_iota(jnp.int32, (slots, toks), 0)
    expert = row // capacity
    hits = [routes_t[k : k + 1, :] == expert for k in range(top)]
    named = sum(h.astype(F32) for h in hits)
    before = (
        lax.broadcasted_iota(jnp.int32, (toks, toks), 0)
        < lax.broadcasted_iota(jnp.int32, (toks, toks), 1)
    ).astype(BF)
    rank = dot(named.astype(BF), before)
    mine = (named > 0.5) & (rank == (row - expert * capacity).astype(F32))
    return mine, hits


def combine_kernel(routes_ref, probs_ref, back_ref, token_ref, prob_ref):
    experts, capacity, wide = back_ref.shape
    slots, width = experts * capacity, token_ref.shape[1]
    mine, hits = places(routes_ref[...], slots, capacity)
    picks = mine.astype(BF)
    n = width // 4
    for i in range(4):
        cols = slice(i * n, (i + 1) * n)
        token_ref[:, cols] = dot_tn(picks, back_ref[:, :, cols].reshape(slots, n)).astype(BF)
    extra = back_ref[:, :, width:].reshape(slots, wide - width)
    value = jnp.sum(extra.astype(F32), axis=1, keepdims=True)
    probs = probs_ref[...]
    for k, hit in enumerate(hits):
        got = jnp.sum(jnp.where(hit & mine, value, 0.0), axis=0, keepdims=True)
        prob_ref[k : k + 1, :] = got / probs[k : k + 1, :]


def open_kernel(
    a_hbm, b_hbm, c_hbm, routes_hbm, probs_hbm, grad_hbm, own_hbm, send_hbm,
    own_ref, routes_ref, probs_ref, grad_ref, send_ref, sems,
):
    n = a_hbm.shape[0]
    experts, capacity, width = send_ref.shape
    shard = start(
        [(r, own_ref.at[pl.ds(i * n, n), :]) for i, r in enumerate((a_hbm, b_hbm, c_hbm))], sems
    )
    small = start(
        [(routes_hbm, routes_ref), (probs_hbm, probs_ref), (grad_hbm, grad_ref)],
        sems.at[pl.ds(3, 3)],
    )
    finish(shard)
    out = start([(own_ref, own_hbm)], sems.at[pl.ds(6, 1)])
    finish(small)
    mine, hits = places(routes_ref[...], experts * capacity, capacity)
    probs = probs_ref[...]
    weight = jnp.zeros(mine.shape, F32)
    for k, hit in enumerate(hits):
        weight = weight + jnp.where(hit, probs[k : k + 1, :], 0.0)
    weight = jnp.where(mine, weight, 0.0)
    high = weight.astype(BF)
    low = (weight - high.astype(F32)).astype(BF)
    for i in range(4):
        cols = slice(i * n, (i + 1) * n)
        rows = dot(high, grad_ref[:, cols]) + dot(low, grad_ref[:, cols])
        send_ref[:, :, cols] = rows.astype(BF).reshape(experts, capacity, n)
    finish(out + start([(send_ref, send_hbm)], sems.at[pl.ds(7, 1)]))


def span(offset, n):
    source = lax.rem(lax.axis_index("dp") + offset, 4)
    return pl.ds(pl.multiple_of(source * n, 128), n)


def pre_kernel(x_hbm, own, far, acc_hbm, x_ref, w_ref, acc_ref, sems):
    n, f = own.shape[0] // 3, own.shape[1]
    moves = []
    for i, (offset, block) in enumerate(((0, own), (2, far))):
        at = pl.ds(i * n, n)
        moves.append((x_hbm.at[:, span(offset, n)], x_ref.at[:, at]))
        moves.append((block.at[pl.ds(0, n), :], w_ref.at[at, pl.ds(0, f)]))
        moves.append((block.at[pl.ds(n, n), :], w_ref.at[at, pl.ds(f, f)]))
    finish(start(moves, sems))
    acc_ref[...] = dot(x_ref[...], w_ref[...])
    finish(start([(acc_ref, acc_hbm)], sems))


def early_kernel(
    x_ref, rows_ref, acc_hbm, own, right, far, acc_out, dh_ref, g_ref, acc_ref, w_ref, wd_ref, sems
):
    slots, n, f = x_ref.shape[0], x_ref.shape[1] // 4, dh_ref.shape[1]
    blocks = ((3, right), (0, own), (2, far))
    moves = [(b.at[pl.ds(2 * n, n), :], wd_ref.at[k]) for k, (_, b) in enumerate(blocks)]
    moves += [(right.at[pl.ds(k * n, n), :], w_ref.at[:, pl.ds(k * f, f)]) for k in (0, 1)]
    moves += [(acc_hbm, acc_ref)]
    copies = start(moves, sems)
    for i in range(4):
        cols = slice(i * n, (i + 1) * n)
        g_ref[:, cols] = rows_ref[:, :, cols].reshape(slots, n)
    finish(copies[0:3])
    dh = None
    for k, (offset, _) in enumerate(blocks):
        term = dot(g_ref[:, span(offset, n)], wd_ref[k])
        dh = term if dh is None else dh + term
    dh_ref[...] = dh
    finish(copies[3:])
    acc_out[...] = acc_ref[...] + dot(x_ref[:, span(3, n)], w_ref[...])


def middle_kernel(
    x_ref, g_ref, acc_ref, dh_ref, own, right, left, far,
    back_hbm, to_own, to_right, to_left, to_far,
    w_ref, wd_ref, back_ref, part_ref, sems,
):
    width, n, f = x_ref.shape[1], x_ref.shape[1] // 4, wd_ref.shape[1]
    slots, shape = x_ref.shape[0], back_ref.shape
    moves = [(left.at[pl.ds(2 * n, n), :], wd_ref)]
    for i, b in ((1, left), (3, right), (0, own), (2, far)):
        moves += [(b.at[pl.ds(k * n, n), :], w_ref.at[span(i, n), pl.ds(k * f, f)]) for k in (0, 1)]
    copies = start(moves, sems)
    last = span(1, n)
    finish(copies[0:3])
    dh = dh_ref[...] + dot(g_ref[:, last], wd_ref[...])
    pre = acc_ref[...] + dot(x_ref[:, last], w_ref[last, :])
    gate, up = pre[:, :f], pre[:, f:]
    sig = jax.nn.sigmoid(gate)
    act = gate * sig
    hidden = act * up
    row_prob = jnp.sum(hidden * dh, axis=1, keepdims=True)
    d_up = (dh * act).astype(BF)
    d_gate = (dh * up * sig * (1.0 + gate * (1.0 - sig))).astype(BF)
    hidden = hidden.astype(BF)
    both = jnp.concatenate([d_gate, d_up], axis=1)
    out = []
    for k, (offset, to) in enumerate(((2, to_far), (1, to_right), (3, to_left), (0, to_own))):
        cols = span(offset, n)
        part = dot_tn(x_ref[:, cols], both).astype(BF)
        part_ref[k, 0:n, :] = part[:, :f]
        part_ref[k, n : 2 * n, :] = part[:, f:]
        part_ref[k, 2 * n :, :] = dot_tn(g_ref[:, cols], hidden).astype(BF)
        out += start([(part_ref.at[k], to)], sems.at[pl.ds(15 + k, 1)])
    finish(copies[3:9])
    for i in range(4):
        at = slice(i * n, (i + 1) * n)
        back_ref[:, :, at] = dot_nt(both, w_ref[at, :]).astype(BF).reshape(*shape[:2], n)
    lane = lax.broadcasted_iota(jnp.int32, (x_ref.shape[0], EXTRA), 1)
    high = row_prob.astype(BF).astype(F32)
    extra = jnp.where(lane == 0, high, jnp.where(lane == 1, row_prob - high, 0.0)).astype(BF)
    back_ref[:, :, width:] = extra.reshape(*shape[:2], EXTRA)
    out += start([(back_ref, back_hbm)], sems.at[pl.ds(19, 1)])
    finish(out)


def first_sum_kernel(own, far, sum_hbm, in_ref, sum_ref, sems):
    finish(start([(own, in_ref.at[0]), (far, in_ref.at[1])], sems))
    sum_ref[...] = in_ref[0].astype(F32) + in_ref[1].astype(F32)
    finish(start([(sum_ref, sum_hbm)], sems))


def last_sum_kernel(sum_ref, a_ref, b_ref, gate_hbm, up_hbm, down_hbm, out_ref, sems):
    n = gate_hbm.shape[0]
    out = []
    for i, hbm in enumerate((gate_hbm, up_hbm, down_hbm)):
        at = pl.ds(i * n, n)
        out_ref[at, :] = (
            sum_ref[at, :] + a_ref[at, :].astype(F32) + b_ref[at, :].astype(F32)
        ).astype(BF)
        out += start([(out_ref.at[at, :], hbm)], sems.at[pl.ds(i, 1)])
    finish(out)


def shift(value, by):
    return lax.ppermute(value, "dp", [(i, (i + by) % 4) for i in range(4)])


def shards(out_grad, routes, gate_probs, saved_inputs, w_gate, w_up, w_down):
    toks, width = out_grad.shape
    experts = lax.axis_size("expert")
    slots = saved_inputs.shape[2]
    capacity = slots // experts
    n, f = w_gate.shape[1], w_gate.shape[2]
    x = saved_inputs[0, 0]
    routes_t, probs_t = routes.T, gate_probs.T
    dma = pltpu.SemaphoreType.DMA
    block = ((3 * n, f), BF)
    row_block = (experts, capacity, width + EXTRA)

    own, send = call(
        open_kernel,
        [block, ((experts, capacity, width), BF)],
        (w_gate[0], w_up[0], w_down[0], routes_t, probs_t, out_grad),
        [
            pltpu.VMEM(*block),
            pltpu.VMEM(routes_t.shape, jnp.int32),
            pltpu.VMEM(probs_t.shape, F32),
            pltpu.VMEM(out_grad.shape, BF),
            pltpu.VMEM((experts, capacity, width), BF),
            dma((8,)),
        ],
    )
    far = shift(own, 2)
    rows = lax.all_to_all(send, "expert", split_axis=0, concat_axis=0, tiled=True)
    left = shift(own, -1)
    right = shift(own, 1)
    (acc,) = call(
        pre_kernel,
        [((slots, 2 * f), F32)],
        (x, own, far),
        [
            pltpu.VMEM((slots, 2 * n), BF),
            pltpu.VMEM((2 * n, 2 * f), BF),
            pltpu.VMEM((slots, 2 * f), F32),
            dma((6,)),
        ],
        flops=PRE_COST,
    )
    acc, dh, g = call(
        early_kernel,
        [((slots, 2 * f), F32), ((slots, f), F32), ((slots, width), BF)],
        (x, rows, acc, own, right, far),
        [
            pltpu.VMEM((slots, 2 * f), F32),
            pltpu.VMEM((n, 2 * f), BF),
            pltpu.VMEM((3, n, f), BF),
            dma((6,)),
        ],
        flops=EARLY_COST,
        where=(pltpu.VMEM,) * 2 + (pltpu.HBM,) * 4 + (pltpu.VMEM,) * 3,
        mib=EARLY_MIB,
    )
    row_grad, to_own, to_right, to_left, to_far = call(
        middle_kernel,
        [(row_block, BF)] + [block] * 4,
        (x, g, acc, dh, own, right, left, far),
        [
            pltpu.VMEM((width, 2 * f), BF),
            pltpu.VMEM((n, f), BF),
            pltpu.VMEM(row_block, BF),
            pltpu.VMEM((4, 3 * n, f), BF),
            dma((20,)),
        ],
        where=(pltpu.VMEM,) * 4 + (pltpu.HBM,) * 9,
        mib=MID_MIB,
    )
    from_far = shift(to_far, 2)
    back = lax.all_to_all(row_grad, "expert", split_axis=0, concat_axis=0, tiled=True)
    from_left = shift(to_right, 1)
    from_right = shift(to_left, -1)
    (total,) = call(
        first_sum_kernel,
        [((3 * n, f), F32)],
        (to_own, from_far),
        [pltpu.VMEM((2, 3 * n, f), BF), pltpu.VMEM((3 * n, f), F32), dma((2,))],
        flops=SUM_COST,
        mib=30,
    )
    grads = call(
        last_sum_kernel,
        [((n, f), BF)] * 3,
        (total, from_left, from_right),
        [pltpu.VMEM((3 * n, f), BF), dma((3,))],
        where=(pltpu.VMEM,) * 3 + (pltpu.HBM,) * 3,
        mib=LAST_MIB,
    )
    token_grad, prob_t = call(
        combine_kernel,
        [((toks, width), BF), (probs_t.shape, F32)],
        (routes_t, probs_t, back),
        where=pltpu.VMEM,
        mib=16,
    )
    return (token_grad, prob_t.T, grads[0][None], grads[1][None], grads[2][None])


def solution(mesh):
    return jax.shard_map(
        shards,
        mesh=mesh,
        in_specs=(
            P(("dp", "expert"), None),
            P(("dp", "expert"), None),
            P(("dp", "expert"), None),
            P("dp", "expert", None, None),
            P("expert", "dp", None),
            P("expert", "dp", None),
            P("expert", "dp", None),
        ),
        out_specs=(
            P(("dp", "expert"), None),
            P(("dp", "expert"), None),
            P("expert", "dp", None),
            P("expert", "dp", None),
            P("expert", "dp", None),
        ),
        check_vma=False,
    )
```

```python
import jax
import jax.numpy as jnp
from jax import lax
from jax.experimental import pallas as pl
from jax.experimental.pallas import tpu as pltpu
from jax.sharding import PartitionSpec as P

TOP = 8
EXTRA = 128
BF = jnp.bfloat16
F32 = jnp.float32
PRE_COST = 12000 << 20
SUM_COST = 12000 << 20
MID_MIB = 52
LAST_MIB = 20


def dot(a, b):
    return jnp.dot(a, b, preferred_element_type=F32)


def dot_nt(a, b):
    return lax.dot_general(a, b, (((1,), (1,)), ((), ())), preferred_element_type=F32)


def dot_tn(a, b):
    return lax.dot_general(a, b, (((0,), (0,)), ((), ())), preferred_element_type=F32)


def call(body, outs, args, scratch=(), flops=0, where=pltpu.HBM, mib=61):
    spaces = where if isinstance(where, tuple) else (where,) * (len(args) + len(outs))
    specs = [pl.BlockSpec(memory_space=space) for space in spaces]
    return pl.pallas_call(
        body,
        out_shape=[jax.ShapeDtypeStruct(s, d) for s, d in outs],
        in_specs=specs[: len(args)],
        out_specs=specs[len(args) :],
        scratch_shapes=list(scratch),
        compiler_params=pltpu.CompilerParams(vmem_limit_bytes=mib * 1024 * 1024),
        cost_estimate=pl.CostEstimate(flops=flops, bytes_accessed=0, transcendentals=0),
    )(*args)


def start(copies, sems):
    made = [pltpu.make_async_copy(a, b, sems.at[i]) for i, (a, b) in enumerate(copies)]
    for c in made:
        c.start()
    return made


def finish(copies):
    for c in copies:
        c.wait()


def places(routes_t, slots, capacity):
    top, toks = routes_t.shape
    row = lax.broadcasted_iota(jnp.int32, (slots, toks), 0)
    expert = row // capacity
    hits = [routes_t[k : k + 1, :] == expert for k in range(top)]
    named = sum(h.astype(F32) for h in hits)
    before = (
        lax.broadcasted_iota(jnp.int32, (toks, toks), 0)
        < lax.broadcasted_iota(jnp.int32, (toks, toks), 1)
    ).astype(BF)
    rank = dot(named.astype(BF), before)
    mine = (named > 0.5) & (rank == (row - expert * capacity).astype(F32))
    return mine, hits


def combine_kernel(routes_ref, probs_ref, back_ref, token_ref, prob_ref):
    experts, capacity, wide = back_ref.shape
    slots, width = experts * capacity, token_ref.shape[1]
    mine, hits = places(routes_ref[...], slots, capacity)
    picks = mine.astype(BF)
    n = width // 4
    for i in range(4):
        cols = slice(i * n, (i + 1) * n)
        token_ref[:, cols] = dot_tn(picks, back_ref[:, :, cols].reshape(slots, n)).astype(BF)
    extra = back_ref[:, :, width:].reshape(slots, wide - width)
    value = jnp.sum(extra.astype(F32), axis=1, keepdims=True)
    probs = probs_ref[...]
    for k, hit in enumerate(hits):
        got = jnp.sum(jnp.where(hit & mine, value, 0.0), axis=0, keepdims=True)
        prob_ref[k : k + 1, :] = got / probs[k : k + 1, :]


def open_kernel(
    a_hbm, b_hbm, c_hbm, routes_hbm, probs_hbm, grad_hbm, own_hbm, send_hbm,
    own_ref, routes_ref, probs_ref, grad_ref, send_ref, sems,
):
    n = a_hbm.shape[0]
    experts, capacity, width = send_ref.shape
    shard = start(
        [(r, own_ref.at[pl.ds(i * n, n), :]) for i, r in enumerate((a_hbm, b_hbm, c_hbm))], sems
    )
    small = start(
        [(routes_hbm, routes_ref), (probs_hbm, probs_ref), (grad_hbm, grad_ref)],
        sems.at[pl.ds(3, 3)],
    )
    finish(shard)
    out = start([(own_ref, own_hbm)], sems.at[pl.ds(6, 1)])
    finish(small)
    mine, hits = places(routes_ref[...], experts * capacity, capacity)
    probs = probs_ref[...]
    weight = jnp.zeros(mine.shape, F32)
    for k, hit in enumerate(hits):
        weight = weight + jnp.where(hit, probs[k : k + 1, :], 0.0)
    weight = jnp.where(mine, weight, 0.0)
    high = weight.astype(BF)
    low = (weight - high.astype(F32)).astype(BF)
    for i in range(4):
        cols = slice(i * n, (i + 1) * n)
        rows = dot(high, grad_ref[:, cols]) + dot(low, grad_ref[:, cols])
        send_ref[:, :, cols] = rows.astype(BF).reshape(experts, capacity, n)
    finish(out + start([(send_ref, send_hbm)], sems.at[pl.ds(7, 1)]))


def span(offset, n):
    source = lax.rem(lax.axis_index("dp") + offset, 4)
    return pl.ds(pl.multiple_of(source * n, 128), n)


def pre_kernel(x_hbm, own, far, acc_hbm, x_ref, w_ref, acc_ref, sems):
    n, f = own.shape[0] // 3, own.shape[1]
    moves = []
    for i, (offset, block) in enumerate(((0, own), (2, far))):
        at = pl.ds(i * n, n)
        moves.append((x_hbm.at[:, span(offset, n)], x_ref.at[:, at]))
        moves.append((block.at[pl.ds(0, n), :], w_ref.at[at, pl.ds(0, f)]))
        moves.append((block.at[pl.ds(n, n), :], w_ref.at[at, pl.ds(f, f)]))
    finish(start(moves, sems))
    acc_ref[...] = dot(x_ref[...], w_ref[...])
    finish(start([(acc_ref, acc_hbm)], sems))


def middle_kernel(
    x_ref, rows_ref, acc_hbm, own, right, left, far,
    back_hbm, to_own, to_right, to_left, to_far,
    acc_ref, w_ref, wd_ref, g_ref, back_ref, part_ref, sems,
):
    width, n, f = x_ref.shape[1], x_ref.shape[1] // 4, wd_ref.shape[1]
    blocks = ((3, right), (1, left), (0, own), (2, far))
    moves = [(b.at[pl.ds(2 * n, n), :], wd_ref.at[span(i, n), :]) for i, b in blocks]
    moves += [(acc_hbm, acc_ref)]
    for i, b in blocks:
        moves += [(b.at[pl.ds(k * n, n), :], w_ref.at[span(i, n), pl.ds(k * f, f)]) for k in (0, 1)]
    copies = start(moves, sems)
    slots, shape = x_ref.shape[0], rows_ref.shape
    for i in range(4):
        cols = slice(i * n, (i + 1) * n)
        g_ref[:, cols] = rows_ref[:, :, cols].reshape(slots, n)
    finish(copies[0:4])
    dh = dot(g_ref[...], wd_ref[...])
    finish(copies[4:9])
    pre = acc_ref[...]
    for offset in (3, 1):
        pre = pre + dot(x_ref[:, span(offset, n)], w_ref[span(offset, n), :])
    gate, up = pre[:, :f], pre[:, f:]
    sig = jax.nn.sigmoid(gate)
    act = gate * sig
    hidden = act * up
    row_prob = jnp.sum(hidden * dh, axis=1, keepdims=True)
    d_up = (dh * act).astype(BF)
    d_gate = (dh * up * sig * (1.0 + gate * (1.0 - sig))).astype(BF)
    hidden = hidden.astype(BF)
    both = jnp.concatenate([d_gate, d_up], axis=1)
    out = []
    for k, (offset, to) in enumerate(((2, to_far), (1, to_right), (3, to_left), (0, to_own))):
        cols = span(offset, n)
        part = dot_tn(x_ref[:, cols], both).astype(BF)
        part_ref[k, 0:n, :] = part[:, :f]
        part_ref[k, n : 2 * n, :] = part[:, f:]
        part_ref[k, 2 * n :, :] = dot_tn(g_ref[:, cols], hidden).astype(BF)
        out += start([(part_ref.at[k], to)], sems.at[pl.ds(15 + k, 1)])
    finish(copies[9:13])
    for i in range(4):
        at = slice(i * n, (i + 1) * n)
        back_ref[:, :, at] = dot_nt(both, w_ref[at, :]).astype(BF).reshape(*shape[:2], n)
    lane = lax.broadcasted_iota(jnp.int32, (x_ref.shape[0], EXTRA), 1)
    high = row_prob.astype(BF).astype(F32)
    extra = jnp.where(lane == 0, high, jnp.where(lane == 1, row_prob - high, 0.0)).astype(BF)
    back_ref[:, :, width:] = extra.reshape(*shape[:2], EXTRA)
    out += start([(back_ref, back_hbm)], sems.at[pl.ds(19, 1)])
    finish(out)


def first_sum_kernel(own, far, sum_hbm, in_ref, sum_ref, sems):
    finish(start([(own, in_ref.at[0]), (far, in_ref.at[1])], sems))
    sum_ref[...] = in_ref[0].astype(F32) + in_ref[1].astype(F32)
    finish(start([(sum_ref, sum_hbm)], sems))


def last_sum_kernel(sum_ref, a_ref, b_ref, gate_hbm, up_hbm, down_hbm, out_ref, sems):
    n = gate_hbm.shape[0]
    out = []
    for i, hbm in enumerate((gate_hbm, up_hbm, down_hbm)):
        at = pl.ds(i * n, n)
        out_ref[at, :] = (
            sum_ref[at, :] + a_ref[at, :].astype(F32) + b_ref[at, :].astype(F32)
        ).astype(BF)
        out += start([(out_ref.at[at, :], hbm)], sems.at[pl.ds(i, 1)])
    finish(out)


def shift(value, by):
    return lax.ppermute(value, "dp", [(i, (i + by) % 4) for i in range(4)])


def shards(out_grad, routes, gate_probs, saved_inputs, w_gate, w_up, w_down):
    toks, width = out_grad.shape
    experts = lax.axis_size("expert")
    slots = saved_inputs.shape[2]
    capacity = slots // experts
    n, f = w_gate.shape[1], w_gate.shape[2]
    x = saved_inputs[0, 0]
    routes_t, probs_t = routes.T, gate_probs.T
    dma = pltpu.SemaphoreType.DMA
    block = ((3 * n, f), BF)
    row_block = (experts, capacity, width + EXTRA)

    own, send = call(
        open_kernel,
        [block, ((experts, capacity, width), BF)],
        (w_gate[0], w_up[0], w_down[0], routes_t, probs_t, out_grad),
        [
            pltpu.VMEM(*block),
            pltpu.VMEM(routes_t.shape, jnp.int32),
            pltpu.VMEM(probs_t.shape, F32),
            pltpu.VMEM(out_grad.shape, BF),
            pltpu.VMEM((experts, capacity, width), BF),
            dma((8,)),
        ],
    )
    far = shift(own, 2)
    rows = lax.all_to_all(send, "expert", split_axis=0, concat_axis=0, tiled=True)
    right = shift(own, 1)
    left = shift(own, -1)
    (acc,) = call(
        pre_kernel,
        [((slots, 2 * f), F32)],
        (x, own, far),
        [
            pltpu.VMEM((slots, 2 * n), BF),
            pltpu.VMEM((2 * n, 2 * f), BF),
            pltpu.VMEM((slots, 2 * f), F32),
            dma((6,)),
        ],
        flops=PRE_COST,
    )
    row_grad, to_own, to_right, to_left, to_far = call(
        middle_kernel,
        [(row_block, BF)] + [block] * 4,
        (x, rows, acc, own, right, left, far),
        [
            pltpu.VMEM((slots, 2 * f), F32),
            pltpu.VMEM((width, 2 * f), BF),
            pltpu.VMEM((width, f), BF),
            pltpu.VMEM((slots, width), BF),
            pltpu.VMEM(row_block, BF),
            pltpu.VMEM((4, 3 * n, f), BF),
            dma((20,)),
        ],
        where=(pltpu.VMEM,) * 2 + (pltpu.HBM,) * 10,
        mib=MID_MIB,
    )
    from_far = shift(to_far, 2)
    back = lax.all_to_all(row_grad, "expert", split_axis=0, concat_axis=0, tiled=True)
    from_left = shift(to_right, 1)
    from_right = shift(to_left, -1)
    (total,) = call(
        first_sum_kernel,
        [((3 * n, f), F32)],
        (to_own, from_far),
        [pltpu.VMEM((2, 3 * n, f), BF), pltpu.VMEM((3 * n, f), F32), dma((2,))],
        flops=SUM_COST,
        mib=30,
    )
    grads = call(
        last_sum_kernel,
        [((n, f), BF)] * 3,
        (total, from_left, from_right),
        [pltpu.VMEM((3 * n, f), BF), dma((3,))],
        where=(pltpu.VMEM,) * 3 + (pltpu.HBM,) * 3,
        mib=LAST_MIB,
    )
    token_grad, prob_t = call(
        combine_kernel,
        [((toks, width), BF), (probs_t.shape, F32)],
        (routes_t, probs_t, back),
        where=pltpu.VMEM,
        mib=16,
    )
    return (token_grad, prob_t.T, grads[0][None], grads[1][None], grads[2][None])


def solution(mesh):
    return jax.shard_map(
        shards,
        mesh=mesh,
        in_specs=(
            P(("dp", "expert"), None),
            P(("dp", "expert"), None),
            P(("dp", "expert"), None),
            P("dp", "expert", None, None),
            P("expert", "dp", None),
            P("expert", "dp", None),
            P("expert", "dp", None),
        ),
        out_specs=(
            P(("dp", "expert"), None),
            P(("dp", "expert"), None),
            P("expert", "dp", None),
            P("expert", "dp", None),
            P("expert", "dp", None),
        ),
        check_vma=False,
    )
```
